512 devices in a mesh: users: 64 (over y, z_lo, core), items: 8 (over x, z_hi).
Axes of the slice: x: 4, y: 4, z: 16 (z_hi: 2, z_lo: 8; z = z_hi * 8 + z_lo), core: 2. Of those that a mesh axis runs over, the one named last changes fastest.
Arguments:
- interactions: bfloat16 [3, 81920, 2048], P(None, 'users', 'items')
- matchings: int32 [3], replicated, may hold values from 1 to 63, as said below
- user_shape: bfloat16 [81920, 128], P('users'), may hold values from 0.5 to 2
- item_shape: bfloat16 [131072, 128], P(('users', 'items')), may hold values from 0.5 to 2
Outputs:
- user_log: bfloat16 [81920, 128], P('users')
- item_log: bfloat16 [131072, 128], P(('users', 'items'))
The draws below stay inside these ranges and needn't reach their ends.
Inputs may be any that keep to these rules, and one draw needn't show every extreme that they name: matchings[0] and matchings[1] are two different values of 1 to 62, and the last matching is 63.
All inputs are finite; a program needn't handle non-finite values.
Results may differ from the reference program's by a relative error of at most 0.0012.
The reference program's roundings to bfloat16 on the way (of `user_exp` and `ratios`) count: a program that leaves them out, or rounds other values in their place, can miss the bound.
Values sent between devices are 32-bit elements; how exact they have to be, the bound alone decides.
A program may use at most 64 MiB of HBM per device.

```python
import math
import jax
import jax.numpy as jnp
from jax import lax

K = 128
U_DEV = 1280
I_BLK = 256
STRATA = 3
USERS = 81920
COLS = 2048
ITEMS = 131072
N_USERS = 64
N_ITEMS = 8


def draw_interactions(key, part):
    count_key = jax.random.fold_in(key, 11)
    heavy_key = jax.random.fold_in(key, 12)
    shape = (STRATA, USERS, COLS)
    counts = jax.random.randint(count_key, shape, 0, 4).astype(jnp.float32)
    heavy = jnp.exp(jax.random.uniform(heavy_key, (1, USERS, 1), jnp.float32, 0.0, math.log(8.0)))
    return (counts * heavy).astype(jnp.bfloat16)


def draw_matchings(key, part):
    key = jax.random.fold_in(key, 21)
    order = jax.random.permutation(key, N_USERS - 2).astype(jnp.int32) + 1
    first_two = order[:2]
    middle = jax.random.randint(jax.random.fold_in(key, 22), (STRATA - 3,), 1, N_USERS).astype(jnp.int32)
    last = jnp.full((1,), N_USERS - 1, jnp.int32)
    return jnp.concatenate([first_two, middle, last]).astype(jnp.int32)


def block_scale(stream_key, shape, shards, low, largest):
    factor_of = 1.0
    for axis_at, shards_of in shards:
        steps = jax.random.uniform(jax.random.fold_in(jax.random.fold_in(stream_key, 6), axis_at), (shards_of,), jnp.float32, low / len(shards), largest / len(shards))
        factor_of = factor_of * jnp.repeat(jnp.exp(steps), shape[axis_at] // shards_of).reshape((-1,) + (1,) * (len(shape) - 1 - axis_at))
    return factor_of


def setup_inputs(seed: int = 0) -> dict:
    key_list = jax.random.split(jax.random.key(seed), 5)
    return {
        "interactions": draw_interactions(jax.random.fold_in(key_list[4], 71), 0),
        "matchings": draw_matchings(jax.random.fold_in(key_list[4], 71), 0),
        "user_shape": jnp.clip(jnp.exp(math.log(2.0) - 1.3862944 * jax.random.uniform(key_list[2], (USERS, K), jnp.float32) ** block_scale(key_list[2], (USERS, K), ((0, 64),), -0.2, 0.2)), 0.5, 2.0).astype(jnp.bfloat16),
        "item_shape": jnp.clip(jnp.exp(math.log(2.0) - 1.3862944 * jax.random.uniform(key_list[3], (ITEMS, K), jnp.float32) ** block_scale(key_list[3], (ITEMS, K), ((0, 512),), -0.2, 0.2)), 0.5, 2.0).astype(jnp.bfloat16),
    }


def expect(shp, rte):
    return lax.digamma(shp) - jnp.log(rte), shp / rte


def per_block(operands):
    user_exp, counts, item_exp = operands
    user_f = user_exp.astype(jnp.float32)
    item_f = item_exp.astype(jnp.float32)
    denominator = jnp.einsum("uk,jik->uji", user_f, item_f)
    ratios = (counts.astype(jnp.float32) / denominator).astype(jnp.bfloat16).astype(jnp.float32)
    user_stat = user_f * jnp.einsum("uji,jik->uk", ratios, item_f)
    item_stat = item_f * jnp.einsum("uji,uk->jik", ratios, user_f)
    return user_stat, item_stat


def reference(interactions, matchings, user_shape, item_shape):
    factor_users = float(N_USERS)
    user_shp = user_shape.astype(jnp.float32).reshape(N_USERS, U_DEV, K)
    user_rte = jnp.ones_like(user_shp)
    item_shp = item_shape.astype(jnp.float32).reshape(N_USERS, N_ITEMS, I_BLK, K)
    item_rte = jnp.ones_like(item_shp)
    for stratum in range(STRATA):
        partner = jnp.bitwise_xor(jnp.arange(N_USERS, dtype=jnp.int32), matchings[stratum].astype(jnp.int32))
        user_elog, user_mean = expect(user_shp, user_rte)
        item_elog, item_mean = expect(item_shp, item_rte)
        user_exp = jnp.exp(user_elog).astype(jnp.bfloat16)
        item_exp = jnp.exp(item_elog).astype(jnp.bfloat16)
        counts = interactions[stratum].reshape(N_USERS, U_DEV, N_ITEMS, I_BLK)
        user_stat, item_stat = lax.map(per_block, (user_exp, counts, item_exp[partner]))
        beta_cols = jnp.sum(item_mean[partner], axis=(1, 2))
        theta_cols = jnp.sum(user_mean, axis=1)
        new_user_shp = 0.5 * user_shp + 0.5 * (0.3 + factor_users * user_stat)
        new_user_rte = 0.5 * user_rte + 0.5 * (0.3 + factor_users * beta_cols[:, None, :])
        item_shp = 0.5 * item_shp + 0.5 * (0.3 + factor_users * item_stat[partner])
        item_rte = 0.5 * item_rte + 0.5 * (0.3 + factor_users * theta_cols[partner][:, None, None, :])
        user_shp, user_rte = new_user_shp, new_user_rte
    user_log = (lax.digamma(user_shp) - jnp.log(user_rte)).reshape(USERS, K).astype(jnp.bfloat16)
    item_log = (lax.digamma(item_shp) - jnp.log(item_rte)).reshape(ITEMS, K).astype(jnp.bfloat16)
    return user_log, item_log
```

```python
import functools

import jax
import jax.numpy as jnp
from jax import lax
from jax.experimental import pallas as pl
from jax.experimental.pallas import tpu as pltpu
from jax.sharding import PartitionSpec as P

MESH = pl.DeviceIdType.MESH
STRATA = 3
UNITS = 128
USERS = 1280
ITEMS = 256
QUARTER = 320
SENT = QUARTER + 8
ROUTED = ITEMS + 8
FACTOR = 64.0
CORE, Z0, Z1, Z2, Y0, Y1 = 1, 2, 4, 8, 16, 32
HOME = 63
ORDER = (Z2, Z1, Z0, Y1, Y0, CORE)


def cotangent(x):
    r = x - jnp.floor(x + 0.5)
    s = r * r
    series = 1.2898681 + s * (
        0.16464647 + s * (0.034686124 + s * (0.0081547124 + s * (0.0019891502 + s * 0.00049217311)))
    )
    return (1.0 - 3.0 * s) / (r * (1.0 - s)) - r * series


def digamma_parts(x, positive=False):
    if positive:
        z = x
    else:
        negative = x <= 0.0
        z = jnp.where(negative, 1.0 - x, x)
    y = z + 4.0
    inverse = 1.0 / y
    square = inverse * inverse
    tail = 0.5 * inverse + square * (
        0.083333333 - square * (0.0083333333 - square * 0.003968254)
    )
    low = jnp.minimum(z, 1e8)
    p = low * (low + 3.0)
    e = -tail - (2.0 * low + 3.0) * (2.0 * p + 2.0) / (p * (p + 2.0))
    if not positive:
        e = jnp.where(negative, e - cotangent(x), e)
    return y, e


def inverse_rate(rte):
    return jnp.where(rte >= 0.0, 1.0 / rte, jnp.nan)


def exp_log(shp, rte, positive=False):
    y, e = digamma_parts(shp, positive)
    return y * inverse_rate(rte) * jnp.exp(e)


def log_mean(shp, rte):
    y, e = digamma_parts(shp)
    return jnp.log(y) + e - jnp.log(rte)


def rows8(row):
    return jnp.broadcast_to(row, (8, UNITS))


def column_sum(value):
    return jnp.sum(value, axis=0, keepdims=True)


def kernel(
    match_ref, inter_hbm, user_ref, item_ref, ulog_ref, ilog_ref,
    inter, route_src, route_dst, rs_src, rs_dst, zh_src, zh_dst, ag_src, ag_dst, fin_src, fin_dst,
    visit, uexp, iexp, istat, ushp,
    load_sem, route_ss, route_rs, rs_ss, rs_rs, zh_ss, zh_rs, ag_ss, ag_rs, fin_ss, fin_rs,
):
    u = lax.axis_index("users")
    i = lax.axis_index("items")
    x = i // 2

    def at_user(mask):
        return (u ^ mask, i)

    def at_x(step):
        return (u, (i + 2 * step) % 8)

    at_zh = (u, i ^ 1)

    loads = [
        pltpu.make_async_copy(inter_hbm.at[s], inter.at[s], load_sem.at[s]) for s in range(STRATA)
    ]
    for load in loads:
        load.start()

    barrier = pltpu.get_barrier_semaphore()
    partners = [at_user(mask) for mask in ORDER + (HOME,)] + [at_x(1), at_x(2), at_x(3), at_zh]
    for partner in partners:
        pl.semaphore_signal(barrier, inc=1, device_id=partner, device_id_type=MESH)

    def remote(src, dst, ss, rs, device):
        return pltpu.make_async_remote_copy(
            src_ref=src, dst_ref=dst, send_sem=ss, recv_sem=rs, device_id=device, device_id_type=MESH
        )

    def route_copy(s, stage):
        return remote(
            route_src.at[s, stage], route_dst.at[s, stage], route_ss.at[s, stage],
            route_rs.at[s, stage], at_user(ORDER[stage]),
        )

    def rs_copy(s, step):
        return remote(
            rs_src.at[s, step], rs_dst.at[s, step - 1], rs_ss.at[s, step - 1],
            rs_rs.at[s, step - 1], at_x(step),
        )

    def zh_copy(s):
        return remote(zh_src.at[s], zh_dst.at[s], zh_ss.at[s], zh_rs.at[s], at_zh)

    def ag_copy(s, step):
        return remote(
            ag_src.at[s], ag_dst.at[s, step - 1], ag_ss.at[s, step - 1], ag_rs.at[s, step - 1],
            at_x(step),
        )

    m0, m1 = match_ref[0], match_ref[1]
    routes = (m0, m0 ^ m1, m1 ^ HOME)

    def route_next(s, stage):
        route_copy(s, stage).wait_recv()
        picked = (routes[s] & ORDER[stage]) != 0
        value = jnp.where(picked, route_dst[s, stage], route_src[s, stage])
        if stage + 1 < len(ORDER):
            route_src[s, stage + 1] = value
            route_copy(s, stage + 1).start()
        else:
            visit[...] = value

    route_src[0, 0, 0:ITEMS] = item_ref[...].astype(jnp.float32)
    route_src[0, 0, ITEMS:] = jnp.ones((8, UNITS), jnp.float32)

    pl.semaphore_wait(barrier, len(partners))
    route_copy(0, 0).start()

    def first_users(d, total):
        rows = pl.ds(((x + d) % 4) * QUARTER, QUARTER)
        shp = user_ref[rows, :].astype(jnp.float32)
        uexp[d] = exp_log(shp, jnp.ones((1, UNITS), jnp.float32), True).astype(jnp.bfloat16)
        return total + column_sum(shp)

    theta = lax.fori_loop(0, 4, first_users, jnp.zeros((1, UNITS), jnp.float32))
    ushp[...] = user_ref[pl.ds(x * QUARTER, QUARTER), :].astype(jnp.float32)
    urte = jnp.ones((1, UNITS), jnp.float32)

    for stage in range(len(ORDER)):
        route_next(0, stage)

    for s in range(STRATA):
        shp = visit[0:ITEMS]
        rte = visit[ITEMS : ITEMS + 1]
        iexp[...] = exp_log(shp, rte).astype(jnp.bfloat16)
        beta = rows8(column_sum(shp) / rte)
        istat[...] = jnp.zeros_like(istat)
        loads[s].wait()

        def users_of(d):
            rows = pl.ds(((x + d) % 4) * QUARTER, QUARTER)
            ue = uexp[d]
            ie = iexp[...]
            denominator = lax.dot_general(
                ue, ie, (((1,), (1,)), ((), ())), preferred_element_type=jnp.float32
            )
            ratios = (inter[s, rows, :].astype(jnp.float32) / denominator).astype(jnp.bfloat16)
            rs_src[s, d, 0:QUARTER] = ue.astype(jnp.float32) * jnp.dot(
                ratios, ie, preferred_element_type=jnp.float32
            )
            rs_src[s, d, QUARTER:] = beta
            istat[...] += lax.dot_general(
                ratios, ue, (((0,), (0,)), ((), ())), preferred_element_type=jnp.float32
            )

        def users_sent(d, carry):
            users_of(d)
            rs_copy(s, d).start()
            return carry

        lax.fori_loop(1, 4, users_sent, 0)
        users_of(0)

        new_shp = 0.5 * shp + 0.5 * (0.3 + FACTOR * (iexp[...].astype(jnp.float32) * istat[...]))
        new_rte = 0.5 * rte + 0.5 * (0.3 + FACTOR * theta)
        last = s == STRATA - 1
        if last:
            fin_src[...] = log_mean(new_shp, new_rte)
            final = remote(fin_src, fin_dst, fin_ss, fin_rs, at_user(HOME))
            final.start()
        else:
            route_src[s + 1, 0, 0:ITEMS] = new_shp
            route_src[s + 1, 0, ITEMS:] = rows8(new_rte)
            route_copy(s + 1, 0).start()

        for step in range(1, 4):
            rs_copy(s, step).wait_recv()
        zh_src[s] = (rs_src[s, 0] + rs_dst[s, 0]) + (rs_dst[s, 1] + rs_dst[s, 2])
        zh_copy(s).start()

        if not last:
            route_next(s + 1, 0)
            route_next(s + 1, 1)

        zh_copy(s).wait_recv()
        total = zh_src[s] + zh_dst[s]
        urte = 0.5 * urte + 0.5 * (0.3 + FACTOR * total[QUARTER : QUARTER + 1])
        own = 0.5 * ushp[...] + 0.5 * (0.3 + FACTOR * total[0:QUARTER])
        ushp[...] = own
        if last:
            result = log_mean(own, urte)
            ag_src[s, 0:QUARTER] = result
            ag_src[s, QUARTER:] = jnp.zeros((8, UNITS), jnp.float32)
        else:
            result = exp_log(own, urte)
            ag_src[s, 0:QUARTER] = result
            ag_src[s, QUARTER:] = rows8(column_sum(own) / urte)
        for step in range(1, 4):
            ag_copy(s, step).start()

        if last:
            final.wait_recv()
            ilog_ref[...] = fin_dst[...].astype(jnp.bfloat16)
            ulog_ref[pl.ds(x * QUARTER, QUARTER), :] = result.astype(jnp.bfloat16)
            for step in range(1, 4):
                ag_copy(s, step).wait_recv()
                rows = pl.ds(((x + 4 - step) % 4) * QUARTER, QUARTER)
                ulog_ref[rows, :] = ag_dst[s, step - 1, 0:QUARTER].astype(jnp.bfloat16)
        else:
            uexp[0] = result.astype(jnp.bfloat16)
            route_next(s + 1, 2)
            route_next(s + 1, 3)
            theta = ag_src[s, QUARTER : QUARTER + 1]
            for step in range(1, 4):
                ag_copy(s, step).wait_recv()
                uexp[4 - step] = ag_dst[s, step - 1, 0:QUARTER].astype(jnp.bfloat16)
                theta = theta + ag_dst[s, step - 1, QUARTER : QUARTER + 1]
            route_next(s + 1, 4)
            route_next(s + 1, 5)

    for s in range(STRATA):
        for stage in range(len(ORDER)):
            route_copy(s, stage).wait_send()
        for step in range(1, 4):
            rs_copy(s, step).wait_send()
            ag_copy(s, step).wait_send()
        zh_copy(s).wait_send()
    final.wait_send()


def per_device(interactions, matchings, user_shape, item_shape):
    stages = len(ORDER)
    f32, dma = jnp.float32, pltpu.SemaphoreType.DMA
    vmem = pl.BlockSpec(memory_space=pltpu.VMEM)
    return pl.pallas_call(
        kernel,
        out_shape=(
            jax.ShapeDtypeStruct((USERS, UNITS), jnp.bfloat16),
            jax.ShapeDtypeStruct((ITEMS, UNITS), jnp.bfloat16),
        ),
        in_specs=[
            pl.BlockSpec(memory_space=pltpu.SMEM),
            pl.BlockSpec(memory_space=pl.ANY),
            vmem,
            vmem,
        ],
        out_specs=(vmem, vmem),
        scratch_shapes=[
            pltpu.VMEM((STRATA, USERS, ITEMS), jnp.bfloat16),
            pltpu.VMEM((STRATA, stages, ROUTED, UNITS), f32),
            pltpu.VMEM((STRATA, stages, ROUTED, UNITS), f32),
            pltpu.VMEM((STRATA, 4, SENT, UNITS), f32),
            pltpu.VMEM((STRATA, 3, SENT, UNITS), f32),
            pltpu.VMEM((STRATA, SENT, UNITS), f32),
            pltpu.VMEM((STRATA, SENT, UNITS), f32),
            pltpu.VMEM((STRATA, SENT, UNITS), f32),
            pltpu.VMEM((STRATA, 3, SENT, UNITS), f32),
            pltpu.VMEM((ITEMS, UNITS), f32),
            pltpu.VMEM((ITEMS, UNITS), f32),
            pltpu.VMEM((ROUTED, UNITS), f32),
            pltpu.VMEM((4, QUARTER, UNITS), jnp.bfloat16),
            pltpu.VMEM((ITEMS, UNITS), jnp.bfloat16),
            pltpu.VMEM((ITEMS, UNITS), f32),
            pltpu.VMEM((QUARTER, UNITS), f32),
            dma((STRATA,)),
            dma((STRATA, stages)),
            dma((STRATA, stages)),
            dma((STRATA, 3)),
            dma((STRATA, 3)),
            dma((STRATA,)),
            dma((STRATA,)),
            dma((STRATA, 3)),
            dma((STRATA, 3)),
            dma,
            dma,
        ],
        compiler_params=pltpu.CompilerParams(
            collective_id=0, has_side_effects=True, vmem_limit_bytes=40 << 20
        ),
        cost_estimate=pl.CostEstimate(
            flops=3 * 6 * USERS * ITEMS * UNITS, bytes_accessed=3 << 20, transcendentals=1 << 20
        ),
    )(matchings, interactions, user_shape, item_shape)


def solution(mesh):
    placed = (P(None, "users", "items"), P(), P("users", None), P(("users", "items"), None))
    return jax.shard_map(
        per_device,
        mesh=mesh,
        in_specs=placed,
        out_specs=(P("users", None), P(("users", "items"), None)),
        check_vma=False,
    )
```

```python
import functools

import jax
import jax.numpy as jnp
from jax import lax
from jax.experimental import pallas as pl
from jax.experimental.pallas import tpu as pltpu
from jax.sharding import PartitionSpec as P

MESH = pl.DeviceIdType.MESH
STRATA = 3
UNITS = 128
USERS = 1280
ITEMS = 256
QUARTER = 320
PIECES = 4
PIECE = QUARTER // PIECES
SENT = QUARTER + 8
ROUTED = ITEMS + 8
FACTOR = 64.0
CORE, Z0, Z1, Z2, Y0, Y1 = 1, 2, 4, 8, 16, 32
HOME = 63
MASKS = (CORE, Z0, Z1, Y0, Y1)
STAGES = len(MASKS) + 1
FAR = Z2
PARTS = (
    (0, 128, (FAR, Z1, Z0, Y1, Y0, CORE)),
    (128, 136, (Y1, Y0, CORE, FAR, Z1, Z0)),
)
STAGE_TIME = {CORE: 1.0, Z0: 2.9, Z1: 3.5, FAR: 7.0, Y0: 2.9, Y1: 3.5}
SCATTERED, SCATTER_STEP, EXCHANGED, EXCHANGE_STEP = 3.0, 1.7, 11.0, 3.5


def cotangent(x):
    r = x - jnp.floor(x + 0.5)
    s = r * r
    series = 1.2898681 + s * (
        0.16464647 + s * (0.034686124 + s * (0.0081547124 + s * (0.0019891502 + s * 0.00049217311)))
    )
    return (1.0 - 3.0 * s) / (r * (1.0 - s)) - r * series


def digamma_parts(x, positive=False):
    if positive:
        z = x
    else:
        negative = x <= 0.0
        z = jnp.where(negative, 1.0 - x, x)
    y = z + 4.0
    inverse = 1.0 / y
    square = inverse * inverse
    tail = 0.5 * inverse + square * (
        0.083333333 - square * (0.0083333333 - square * 0.003968254)
    )
    low = jnp.minimum(z, 1e8)
    p = low * (low + 3.0)
    e = -tail - (2.0 * low + 3.0) * (2.0 * p + 2.0) / (p * (p + 2.0))
    if not positive:
        e = jnp.where(negative, e - cotangent(x), e)
    return y, e


def inverse_rate(rte):
    return jnp.where(rte >= 0.0, 1.0 / rte, jnp.nan)


def exp_log(shp, rte, positive=False):
    y, e = digamma_parts(shp, positive)
    return y * inverse_rate(rte) * jnp.exp(e)


def log_mean(shp, rte):
    y, e = digamma_parts(shp)
    return jnp.log(y) + e - jnp.log(rte)


def in_rows(count, step, body):
    def once(n, carry):
        body(pl.ds(pl.multiple_of(n * step, step), step))
        return carry

    lax.fori_loop(0, count // step, once, 0)


def rows8(row):
    return jnp.broadcast_to(row, (8, UNITS))


def column_sum(value):
    return jnp.sum(value, axis=0, keepdims=True)


def kernel(
    far, match_hbm, inter_hbm, user_hbm, item_hbm, ulog_ref, ilog_ref,
    match_ref, inter, user_ref, item_ref,
    route_src, route_dst, rs_src, rs_dst, zh_src, zh_dst, ag_src, ag_dst, fin_src, fin_dst,
    visit, uexp, iexp, istat, ushp,
    load_sem, route_ss, route_rs, rs_ss, rs_rs, zh_ss, zh_rs, ag_ss, ag_rs, fin_ss, fin_rs,
):
    u = lax.axis_index("users")
    i = lax.axis_index("items")
    x = i // 2

    def at_user(mask):
        return (u ^ mask, i)

    def at_x(step):
        return (u, (i + 2 * step) % 8)

    at_zh = (u, i ^ 1)

    barrier = pltpu.get_barrier_semaphore()
    moves = MASKS + (HOME,) + tuple(sorted(set(far) - {0}))
    partners = [at_user(mask) for mask in moves] + [at_x(1), at_x(2), at_x(3), at_zh]
    for partner in partners:
        pl.semaphore_signal(barrier, inc=1, device_id=partner, device_id_type=MESH)

    load_item = pltpu.make_async_copy(item_hbm, item_ref, load_sem.at[STRATA])
    load_user = pltpu.make_async_copy(user_hbm, user_ref, load_sem.at[STRATA + 1])
    load_match = pltpu.make_async_copy(match_hbm, match_ref, load_sem.at[STRATA + 2])
    loads = [
        pltpu.make_async_copy(inter_hbm.at[s], inter.at[s], load_sem.at[s]) for s in range(STRATA)
    ]
    for load in [load_item, load_match, load_user] + loads:
        load.start()

    def remote(src, dst, ss, rs, device):
        return pltpu.make_async_remote_copy(
            src_ref=src, dst_ref=dst, send_sem=ss, recv_sem=rs, device_id=device, device_id_type=MESH
        )

    def route_part(s, part):
        first, rows, order = PARTS[part]
        masks = tuple(far[s] if mask == FAR else mask for mask in order)
        return first, rows, tuple(mask for mask in masks if mask)

    def route_copy(s, part, stage):
        first, rows, order = route_part(s, part)
        rows = pl.ds(first, rows)
        return remote(
            route_src.at[s, stage, rows], route_dst.at[s, stage, rows], route_ss.at[s],
            route_rs.at[s, part, stage], at_user(order[stage]),
        )

    def rs_rows(piece):
        return pl.ds(8 + piece * PIECE, PIECE) if piece else pl.ds(0, 8 + PIECE)

    def rs_copy(s, step, piece):
        rows = rs_rows(piece)
        return remote(
            rs_src.at[s, step, rows], rs_dst.at[s, step - 1, rows], rs_ss.at[s],
            rs_rs.at[s, piece], at_x(step),
        )

    def zh_copy(s, piece):
        rows = rs_rows(piece)
        return remote(
            zh_src.at[s, rows], zh_dst.at[s, rows], zh_ss.at[s], zh_rs.at[s, piece], at_zh
        )

    def ag_copy(s, step, piece):
        more = 8 if piece == PIECES - 1 else 0
        rows = pl.ds(piece * PIECE, PIECE + more)
        return remote(
            ag_src.at[s, rows], ag_dst.at[s, step - 1, rows], ag_ss.at[s], ag_rs.at[s], at_x(step),
        )

    def wait_bytes(ref, sem):
        pltpu.make_async_copy(ref, ref, sem).wait()

    def routed(s):
        events = []
        for part in range(len(PARTS)):
            at = 0.0
            for stage, mask in enumerate(route_part(s, part)[2]):
                at += STAGE_TIME[mask]
                events.append((at, functools.partial(route_next, s, part, stage)))
        return events

    def run(events):
        for _, event in sorted(events, key=lambda timed: timed[0]):
            event()

    def route_next(s, part, stage):
        first, rows, order = route_part(s, part)
        rows = pl.ds(first, rows)
        route_copy(s, part, stage).wait_recv()
        if order[stage] & FAR:
            value = route_dst[s, stage, rows]
        else:
            m0, m1 = match_ref[0], match_ref[1]
            mask = (m0, m0 ^ m1, m1 ^ HOME)[s]
            picked = (mask & order[stage]) != 0
            value = jnp.where(picked, route_dst[s, stage, rows], route_src[s, stage, rows])
        if stage + 1 < len(order):
            route_src[s, stage + 1, rows] = value
            route_copy(s, part, stage + 1).start()
        else:
            visit[rows] = value

    load_item.wait()
    route_src[0, 0, 0:ITEMS] = item_ref[...].astype(jnp.float32)
    route_src[0, 0, ITEMS:] = jnp.ones((8, UNITS), jnp.float32)
    load_match.wait()
    load_user.wait()

    pl.semaphore_wait(barrier, len(partners))
    for part in range(len(PARTS)):
        route_copy(0, part, 0).start()

    def first_users(d, total):
        rows = pl.ds(((x + d) % 4) * QUARTER, QUARTER)
        shp = user_ref[rows, :].astype(jnp.float32)
        uexp[d] = exp_log(shp, jnp.ones((1, UNITS), jnp.float32), True).astype(jnp.bfloat16)
        return total + column_sum(shp)

    theta = lax.fori_loop(0, 4, first_users, jnp.zeros((1, UNITS), jnp.float32))
    ushp[...] = user_ref[pl.ds(x * QUARTER, QUARTER), :].astype(jnp.float32)
    urte = jnp.ones((1, UNITS), jnp.float32)

    run(routed(0))

    for s in range(STRATA):
        last = s == STRATA - 1
        rte = visit[ITEMS : ITEMS + 1]

        def item_rows(rows):
            iexp[rows] = exp_log(visit[rows], rte).astype(jnp.bfloat16)

        in_rows(ITEMS, 64, item_rows)
        rs_src[s, :, 0:8] = jnp.broadcast_to(column_sum(visit[0:ITEMS]) / rte, (4, 8, UNITS))
        istat[...] = jnp.zeros_like(istat)
        loads[s].wait()

        def users_of(d, first, rows):
            weights = inter[s, pl.ds(((x + d) % 4) * QUARTER + first, rows), :]
            ue = uexp[d, first : first + rows]
            ie = iexp[...]
            denominator = lax.dot_general(
                ue, ie, (((1,), (1,)), ((), ())), preferred_element_type=jnp.float32
            )
            ratios = (weights.astype(jnp.float32) / denominator).astype(jnp.bfloat16)
            rs_src[s, d, 8 + first : 8 + first + rows] = ue.astype(jnp.float32) * jnp.dot(
                ratios, ie, preferred_element_type=jnp.float32
            )
            istat[...] += lax.dot_general(
                ratios, ue, (((0,), (0,)), ((), ())), preferred_element_type=jnp.float32
            )

        for half in range(2):
            def users_sent(n, carry, half=half):
                d = (n + 1) % 4
                users_of(d, half * (QUARTER // 2), QUARTER // 2)

                @pl.when(n < 3)
                def _():
                    for piece in range(half * PIECES // 2, (half + 1) * PIECES // 2):
                        rs_copy(s, n + 1, piece).start()

                return carry

            lax.fori_loop(0, 4, users_sent, 0)

        new_rte = 0.5 * rte + 0.5 * (0.3 + FACTOR * theta)

        def new_rows(rows):
            stat = iexp[rows].astype(jnp.float32) * istat[rows]
            shp = 0.5 * visit[rows] + 0.5 * (0.3 + FACTOR * stat)
            if last:
                fin_src[rows] = log_mean(shp, new_rte)
            else:
                route_src[s + 1, 0, rows] = shp

        in_rows(ITEMS, 64, new_rows)
        if last:
            final = remote(fin_src, fin_dst, fin_ss, fin_rs, at_user(HOME))
            final.start()
        else:
            route_src[s + 1, 0, ITEMS:] = rows8(new_rte)
            for part in range(len(PARTS)):
                route_copy(s + 1, part, 0).start()

        state = {"urte": urte, "columns": jnp.zeros((1, UNITS), jnp.float32)}

        def scattered(piece):
            rows = rs_rows(piece)
            wait_bytes(rs_dst.at[s, :, rows], rs_rs.at[s, piece])
            zh_src[s, rows] = (rs_src[s, 0, rows] + rs_dst[s, 0, rows]) + (
                rs_dst[s, 1, rows] + rs_dst[s, 2, rows]
            )
            zh_copy(s, piece).start()

        def exchanged(piece):
            zh_copy(s, piece).wait_recv()
            if piece == 0:
                beta = zh_src[s, 0:1] + zh_dst[s, 0:1]
                state["urte"] = 0.5 * state["urte"] + 0.5 * (0.3 + FACTOR * beta)
            mine = pl.ds(piece * PIECE, PIECE)
            stat = pl.ds(8 + piece * PIECE, PIECE)
            own = 0.5 * ushp[mine] + 0.5 * (0.3 + FACTOR * (zh_src[s, stat] + zh_dst[s, stat]))
            ushp[mine] = own
            if last:
                ag_src[s, mine] = log_mean(own, state["urte"])
            else:
                ag_src[s, mine] = exp_log(own, state["urte"])
                state["columns"] += column_sum(own)
            if piece == PIECES - 1:
                ag_src[s, QUARTER:] = rows8(state["columns"] / state["urte"])
            for step in range(1, 4):
                ag_copy(s, step, piece).start()

        events = [] if last else routed(s + 1)
        for piece in range(PIECES):
            events.append((SCATTERED + piece * SCATTER_STEP, functools.partial(scattered, piece)))
            events.append((EXCHANGED + piece * EXCHANGE_STEP, functools.partial(exchanged, piece)))
        run(events)
        urte = state["urte"]

        if last:
            final.wait_recv()
            ilog_ref[...] = fin_dst[...].astype(jnp.bfloat16)
            ulog_ref[pl.ds(x * QUARTER, QUARTER), :] = ag_src[s, 0:QUARTER].astype(jnp.bfloat16)
        else:
            uexp[0] = ag_src[s, 0:QUARTER].astype(jnp.bfloat16)
            theta = ag_src[s, QUARTER : QUARTER + 1]
        wait_bytes(ag_dst.at[s], ag_rs.at[s])
        for step in range(1, 4):
            value = ag_dst[s, step - 1, 0:QUARTER].astype(jnp.bfloat16)
            if last:
                ulog_ref[pl.ds(((x + 4 - step) % 4) * QUARTER, QUARTER), :] = value
            else:
                uexp[4 - step] = value
                theta = theta + ag_dst[s, step - 1, QUARTER : QUARTER + 1]

    for s in range(STRATA):
        wait_bytes(route_src.at[s, 0 : len(route_part(s, 0)[2])], route_ss.at[s])
        wait_bytes(rs_src.at[s, 1:4], rs_ss.at[s])
        wait_bytes(zh_src.at[s], zh_ss.at[s])
        wait_bytes(ag_dst.at[s], ag_ss.at[s])
    final.wait_send()


def call(far, number, interactions, matchings, user_shape, item_shape):
    f32, dma = jnp.float32, pltpu.SemaphoreType.DMA
    vmem = pl.BlockSpec(memory_space=pltpu.VMEM)
    hbm = pl.BlockSpec(memory_space=pltpu.HBM)
    return pl.pallas_call(
        functools.partial(kernel, far),
        out_shape=(
            jax.ShapeDtypeStruct((USERS, UNITS), jnp.bfloat16),
            jax.ShapeDtypeStruct((ITEMS, UNITS), jnp.bfloat16),
        ),
        in_specs=[hbm, hbm, hbm, hbm],
        out_specs=(vmem, vmem),
        scratch_shapes=[
            pltpu.SMEM((STRATA,), jnp.int32),
            pltpu.VMEM((STRATA, USERS, ITEMS), jnp.bfloat16),
            pltpu.VMEM((USERS, UNITS), jnp.bfloat16),
            pltpu.VMEM((ITEMS, UNITS), jnp.bfloat16),
            pltpu.VMEM((STRATA, STAGES, ROUTED, UNITS), f32),
            pltpu.VMEM((STRATA, STAGES, ROUTED, UNITS), f32),
            pltpu.VMEM((STRATA, 4, SENT, UNITS), f32),
            pltpu.VMEM((STRATA, 3, SENT, UNITS), f32),
            pltpu.VMEM((STRATA, SENT, UNITS), f32),
            pltpu.VMEM((STRATA, SENT, UNITS), f32),
            pltpu.VMEM((STRATA, SENT, UNITS), f32),
            pltpu.VMEM((STRATA, 3, SENT, UNITS), f32),
            pltpu.VMEM((ITEMS, UNITS), f32),
            pltpu.VMEM((ITEMS, UNITS), f32),
            pltpu.VMEM((ROUTED, UNITS), f32),
            pltpu.VMEM((4, QUARTER, UNITS), jnp.bfloat16),
            pltpu.VMEM((ITEMS, UNITS), jnp.bfloat16),
            pltpu.VMEM((ITEMS, UNITS), f32),
            pltpu.VMEM((QUARTER, UNITS), f32),
            dma((STRATA + 3,)),
            dma((STRATA,)),
            dma((STRATA, len(PARTS), STAGES)),
            dma((STRATA,)),
            dma((STRATA, PIECES)),
            dma((STRATA,)),
            dma((STRATA, PIECES)),
            dma((STRATA,)),
            dma((STRATA,)),
            dma,
            dma,
        ],
        compiler_params=pltpu.CompilerParams(
            collective_id=number, has_side_effects=True, vmem_limit_bytes=63 << 20
        ),
        cost_estimate=pl.CostEstimate(
            flops=3 * 6 * USERS * ITEMS * UNITS, bytes_accessed=3 << 20, transcendentals=1 << 20
        ),
    )(matchings, interactions, user_shape, item_shape)


def per_device(interactions, matchings, user_shape, item_shape):
    calls = []
    for first in range(2):
        for second in range(2):
            far = (first * FAR, (first ^ second) * FAR, (second ^ 1) * FAR)
            calls.append(functools.partial(call, far, len(calls)))
    bits = (matchings // FAR) & 1
    return lax.switch(
        bits[0] * 2 + bits[1], calls, interactions, matchings, user_shape, item_shape
    )


def solution(mesh):
    placed = (P(None, "users", "items"), P(), P("users", None), P(("users", "items"), None))
    return jax.shard_map(
        per_device,
        mesh=mesh,
        in_specs=placed,
        out_specs=(P("users", None), P(("users", "items"), None)),
        check_vma=False,
    )
```

```python
import functools

import jax
import jax.numpy as jnp
from jax import lax
from jax.experimental import pallas as pl
from jax.experimental.pallas import tpu as pltpu
from jax.sharding import PartitionSpec as P

MESH = pl.DeviceIdType.MESH
STRATA = 3
UNITS = 128
USERS = 1280
ITEMS = 256
QUARTER = 320
PIECES = 4
PIECE = QUARTER // PIECES
SENT = QUARTER + 8
ROUTED = ITEMS + 8
FACTOR = 64.0
CORE, Z0, Z1, Z2, Y0, Y1 = 1, 2, 4, 8, 16, 32
HOME = 63
Y = Y0 | Y1
MASKS = (CORE, Z0, Z1, Y0, Y1, Y)
STAGES = 5
SLOTS = STAGES + 2
FAR = Z2
PARTS = (
    (0, 128, (FAR, Z1, Z0, Y, CORE)),
    (128, 136, (Y, CORE, FAR, Z1, Z0)),
)
STAGE_TIME = {CORE: 1.5, Z0: 4.4, Z1: 5.2, FAR: 10.5, Y: 7.5}
SCATTERED, SCATTER_STEP, EXCHANGED, EXCHANGE_STEP = 3.0, 1.7, 11.0, 3.5


def cotangent(x):
    r = x - jnp.floor(x + 0.5)
    s = r * r
    series = 1.2898681 + s * (
        0.16464647 + s * (0.034686124 + s * (0.0081547124 + s * (0.0019891502 + s * 0.00049217311)))
    )
    return (1.0 - 3.0 * s) / (r * (1.0 - s)) - r * series


def digamma_parts(x, positive=False):
    if positive:
        z = x
    else:
        negative = x <= 0.0
        z = jnp.where(negative, 1.0 - x, x)
    y = z + 4.0
    inverse = 1.0 / y
    square = inverse * inverse
    tail = 0.5 * inverse + square * (
        0.083333333 - square * (0.0083333333 - square * 0.003968254)
    )
    low = jnp.minimum(z, 1e8)
    p = low * (low + 3.0)
    e = -tail - (2.0 * low + 3.0) * (2.0 * p + 2.0) / (p * (p + 2.0))
    if not positive:
        e = jnp.where(negative, e - cotangent(x), e)
    return y, e


def inverse_rate(rte):
    return jnp.where(rte >= 0.0, 1.0 / rte, jnp.nan)


def exp_log(shp, rte, positive=False):
    y, e = digamma_parts(shp, positive)
    return y * inverse_rate(rte) * jnp.exp(e)


def log_mean(shp, rte):
    y, e = digamma_parts(shp)
    return jnp.log(y) + e - jnp.log(rte)


def in_rows(count, step, body):
    def once(n, carry):
        body(pl.ds(pl.multiple_of(n * step, step), step))
        return carry

    lax.fori_loop(0, count // step, once, 0)


def rows8(row):
    return jnp.broadcast_to(row, (8, UNITS))


def column_sum(value):
    return jnp.sum(value, axis=0, keepdims=True)


def kernel(
    far, match_hbm, inter_hbm, user_hbm, item_hbm, ulog_ref, ilog_ref,
    match_ref, inter, user_ref, item_ref,
    route_src, route_dst, rs_src, rs_dst, zh_src, zh_dst, ag_src, ag_dst, fin_src, fin_dst,
    visit, uexp, iexp, istat, ushp,
    load_sem, route_ss, route_rs, rs_ss, rs_rs, zh_ss, zh_rs, ag_ss, ag_rs, fin_ss, fin_rs,
):
    u = lax.axis_index("users")
    i = lax.axis_index("items")
    x = i // 2

    def at_user(mask):
        return (u ^ mask, i)

    def at_x(step):
        return (u, (i + 2 * step) % 8)

    at_zh = (u, i ^ 1)

    barrier = pltpu.get_barrier_semaphore()
    moves = MASKS + (HOME,) + tuple(sorted(set(far) - {0, Z1}))
    partners = [at_user(mask) for mask in moves] + [at_x(1), at_x(2), at_x(3), at_zh]
    for partner in partners:
        pl.semaphore_signal(barrier, inc=1, device_id=partner, device_id_type=MESH)

    load_item = pltpu.make_async_copy(item_hbm, item_ref, load_sem.at[STRATA])
    load_user = pltpu.make_async_copy(user_hbm, user_ref, load_sem.at[STRATA + 1])
    load_match = pltpu.make_async_copy(match_hbm, match_ref, load_sem.at[STRATA + 2])
    loads = [
        pltpu.make_async_copy(inter_hbm.at[s], inter.at[s], load_sem.at[s]) for s in range(STRATA)
    ]
    for load in [load_item, load_match, load_user] + loads:
        load.start()

    def remote(src, dst, ss, rs, device):
        return pltpu.make_async_remote_copy(
            src_ref=src, dst_ref=dst, send_sem=ss, recv_sem=rs, device_id=device, device_id_type=MESH
        )

    def route_part(s, part):
        first, rows, order = PARTS[part]
        masks = tuple(far[s] if mask == FAR else mask for mask in order if s or mask != Z1)
        return first, rows, tuple(mask for mask in masks if mask)

    def known(s, mask):
        return mask & (FAR if s else FAR | Z1)

    def route_copies(s, part, stage):
        first, rows, order = route_part(s, part)
        rows = pl.ds(first, rows)
        masks = (Y0, Y1, Y) if order[stage] == Y else (order[stage],)
        slots = (stage, STAGES, STAGES + 1)
        return [
            remote(
                route_src.at[s, stage, rows], route_dst.at[s, slot, rows], route_ss.at[s],
                route_rs.at[s, part, slot], at_user(mask),
            )
            for mask, slot in zip(masks, slots)
        ]

    def route_start(s, part, stage):
        for copy in route_copies(s, part, stage):
            copy.start()

    def rs_rows(piece):
        return pl.ds(8 + piece * PIECE, PIECE) if piece else pl.ds(0, 8 + PIECE)

    def rs_copy(s, step, piece):
        rows = rs_rows(piece)
        return remote(
            rs_src.at[s, step, rows], rs_dst.at[s, step - 1, rows], rs_ss.at[s],
            rs_rs.at[s, piece], at_x(step),
        )

    def zh_copy(s, piece):
        rows = rs_rows(piece)
        return remote(
            zh_src.at[s, rows], zh_dst.at[s, rows], zh_ss.at[s], zh_rs.at[s, piece], at_zh
        )

    def ag_copy(s, step, piece):
        more = 8 if piece == PIECES - 1 else 0
        rows = pl.ds(piece * PIECE, PIECE + more)
        return remote(
            ag_src.at[s, rows], ag_dst.at[s, step - 1, rows], ag_ss.at[s], ag_rs.at[s], at_x(step),
        )

    def wait_bytes(ref, sem):
        pltpu.make_async_copy(ref, ref, sem).wait()

    def routed(s):
        events = []
        for part in range(len(PARTS)):
            at = 0.0
            for stage, mask in enumerate(route_part(s, part)[2]):
                at += STAGE_TIME.get(mask, STAGE_TIME[FAR])
                events.append((at, functools.partial(route_next, s, part, stage)))
        return events

    def run(events):
        for _, event in sorted(events, key=lambda timed: timed[0]):
            event()

    def route_next(s, part, stage):
        first, rows, order = route_part(s, part)
        rows = pl.ds(first, rows)
        for copy in route_copies(s, part, stage):
            copy.wait_recv()
        if known(s, order[stage]):
            value = route_dst[s, stage, rows]
        else:
            m0, m1 = match_ref[0], match_ref[1]
            mask = (m0, m0 ^ m1, m1 ^ HOME)[s]
            picked = mask & order[stage]
            value = jnp.where(picked != 0, route_dst[s, stage, rows], route_src[s, stage, rows])
            if order[stage] == Y:
                value = jnp.where(picked == Y1, route_dst[s, STAGES, rows], value)
                value = jnp.where(picked == Y, route_dst[s, STAGES + 1, rows], value)
        if stage + 1 < len(order):
            route_src[s, stage + 1, rows] = value
            route_start(s, part, stage + 1)
        else:
            visit[rows] = value

    load_item.wait()
    route_src[0, 0, 0:ITEMS] = item_ref[...].astype(jnp.float32)
    route_src[0, 0, ITEMS:] = jnp.ones((8, UNITS), jnp.float32)
    load_match.wait()
    load_user.wait()

    pl.semaphore_wait(barrier, len(partners))
    for part in range(len(PARTS)):
        route_start(0, part, 0)

    def first_users(n, total):
        d, first = n // 5, pl.multiple_of((n % 5) * 64, 64)
        shp = user_ref[pl.ds(((x + d) % 4) * QUARTER + first, 64), :].astype(jnp.float32)
        uexp[d, pl.ds(first, 64)] = exp_log(
            shp, jnp.ones((1, UNITS), jnp.float32), True
        ).astype(jnp.bfloat16)
        return total + column_sum(shp)

    theta = lax.fori_loop(0, 20, first_users, jnp.zeros((1, UNITS), jnp.float32))
    ushp[...] = user_ref[pl.ds(x * QUARTER, QUARTER), :].astype(jnp.float32)
    urte = jnp.ones((1, UNITS), jnp.float32)

    run(routed(0))

    for s in range(STRATA):
        last = s == STRATA - 1
        rte = visit[ITEMS : ITEMS + 1]

        def item_rows(rows):
            iexp[rows] = exp_log(visit[rows], rte).astype(jnp.bfloat16)

        in_rows(ITEMS, 64, item_rows)
        rs_src[s, :, 0:8] = jnp.broadcast_to(column_sum(visit[0:ITEMS]) / rte, (4, 8, UNITS))
        istat[...] = jnp.zeros_like(istat)
        loads[s].wait()

        def users_of(d, first, rows):
            weights = inter[s, pl.ds(((x + d) % 4) * QUARTER + first, rows), :]
            ue = uexp[d, pl.ds(first, rows)]
            ie = iexp[...]
            denominator = lax.dot_general(
                ue, ie, (((1,), (1,)), ((), ())), preferred_element_type=jnp.float32
            )
            ratios = (weights.astype(jnp.float32) / denominator).astype(jnp.bfloat16)
            rs_src[s, d, pl.ds(8 + first, rows)] = ue.astype(jnp.float32) * jnp.dot(
                ratios, ie, preferred_element_type=jnp.float32
            )
            istat[...] += lax.dot_general(
                ratios, ue, (((0,), (0,)), ((), ())), preferred_element_type=jnp.float32
            )

        def users_sent(n, carry):
            d, half = (n + 1) % 4, n // 4
            users_of(d, pl.multiple_of(half * (QUARTER // 2), 32), QUARTER // 2)
            for step in range(2):
                @pl.when((d > 0) & (half == step))
                def _(step=step):
                    for piece in range(step * PIECES // 2, (step + 1) * PIECES // 2):
                        rs_copy(s, d, piece).start()

            return carry

        lax.fori_loop(0, 8, users_sent, 0)

        new_rte = 0.5 * rte + 0.5 * (0.3 + FACTOR * theta)

        def new_rows(rows):
            stat = iexp[rows].astype(jnp.float32) * istat[rows]
            shp = 0.5 * visit[rows] + 0.5 * (0.3 + FACTOR * stat)
            if last:
                fin_src[rows] = log_mean(shp, new_rte)
            else:
                route_src[s + 1, 0, rows] = shp

        in_rows(ITEMS, 64, new_rows)
        if last:
            final = remote(fin_src, fin_dst, fin_ss, fin_rs, at_user(HOME))
            final.start()
        else:
            route_src[s + 1, 0, ITEMS:] = rows8(new_rte)
            for part in range(len(PARTS)):
                route_start(s + 1, part, 0)

        state = {"urte": urte, "columns": jnp.zeros((1, UNITS), jnp.float32)}

        def scattered(piece):
            rows = rs_rows(piece)
            wait_bytes(rs_dst.at[s, :, rows], rs_rs.at[s, piece])
            zh_src[s, rows] = (rs_src[s, 0, rows] + rs_dst[s, 0, rows]) + (
                rs_dst[s, 1, rows] + rs_dst[s, 2, rows]
            )
            zh_copy(s, piece).start()

        def exchanged(piece):
            zh_copy(s, piece).wait_recv()
            if piece == 0:
                beta = zh_src[s, 0:1] + zh_dst[s, 0:1]
                state["urte"] = 0.5 * state["urte"] + 0.5 * (0.3 + FACTOR * beta)
            step = PIECE // 2

            def own_rows(n, columns):
                at = pl.multiple_of(piece * PIECE + n * step, 8)
                mine, stat = pl.ds(at, step), pl.ds(at + 8, step)
                total = zh_src[s, stat] + zh_dst[s, stat]
                own = 0.5 * ushp[mine] + 0.5 * (0.3 + FACTOR * total)
                ushp[mine] = own
                ag_src[s, mine] = (log_mean if last else exp_log)(own, state["urte"])
                return columns + column_sum(own)

            state["columns"] = lax.fori_loop(0, 2, own_rows, state["columns"])
            if piece == PIECES - 1:
                ag_src[s, QUARTER:] = rows8(state["columns"] / state["urte"])
            for step in range(1, 4):
                ag_copy(s, step, piece).start()

        events = [] if last else routed(s + 1)
        for piece in range(PIECES):
            events.append((SCATTERED + piece * SCATTER_STEP, functools.partial(scattered, piece)))
            events.append((EXCHANGED + piece * EXCHANGE_STEP, functools.partial(exchanged, piece)))
        run(events)
        urte = state["urte"]

        if last:
            final.wait_recv()
            ilog_ref[...] = fin_dst[...].astype(jnp.bfloat16)
            ulog_ref[pl.ds(x * QUARTER, QUARTER), :] = ag_src[s, 0:QUARTER].astype(jnp.bfloat16)
        else:
            uexp[0] = ag_src[s, 0:QUARTER].astype(jnp.bfloat16)
            theta = ag_src[s, QUARTER : QUARTER + 1]
        wait_bytes(ag_dst.at[s], ag_rs.at[s])
        for step in range(1, 4):
            value = ag_dst[s, step - 1, 0:QUARTER].astype(jnp.bfloat16)
            if last:
                ulog_ref[pl.ds(((x + 4 - step) % 4) * QUARTER, QUARTER), :] = value
            else:
                uexp[4 - step] = value
                theta = theta + ag_dst[s, step - 1, QUARTER : QUARTER + 1]

    for s in range(STRATA):
        wait_bytes(route_dst.at[s, 0 : len(route_part(s, 0)[2]) + 2], route_ss.at[s])
        wait_bytes(rs_src.at[s, 1:4], rs_ss.at[s])
        wait_bytes(zh_src.at[s], zh_ss.at[s])
        wait_bytes(ag_dst.at[s], ag_ss.at[s])
    final.wait_send()


def call(far, number, interactions, matchings, user_shape, item_shape):
    f32, dma = jnp.float32, pltpu.SemaphoreType.DMA
    vmem = pl.BlockSpec(memory_space=pltpu.VMEM)
    hbm = pl.BlockSpec(memory_space=pltpu.HBM)
    return pl.pallas_call(
        functools.partial(kernel, far),
        out_shape=(
            jax.ShapeDtypeStruct((USERS, UNITS), jnp.bfloat16),
            jax.ShapeDtypeStruct((ITEMS, UNITS), jnp.bfloat16),
        ),
        in_specs=[hbm, hbm, hbm, hbm],
        out_specs=(vmem, vmem),
        scratch_shapes=[
            pltpu.SMEM((STRATA,), jnp.int32),
            pltpu.VMEM((STRATA, USERS, ITEMS), jnp.bfloat16),
            pltpu.VMEM((USERS, UNITS), jnp.bfloat16),
            pltpu.VMEM((ITEMS, UNITS), jnp.bfloat16),
            pltpu.VMEM((STRATA, STAGES, ROUTED, UNITS), f32),
            pltpu.VMEM((STRATA, SLOTS, ROUTED, UNITS), f32),
            pltpu.VMEM((STRATA, 4, SENT, UNITS), f32),
            pltpu.VMEM((STRATA, 3, SENT, UNITS), f32),
            pltpu.VMEM((STRATA, SENT, UNITS), f32),
            pltpu.VMEM((STRATA, SENT, UNITS), f32),
            pltpu.VMEM((STRATA, SENT, UNITS), f32),
            pltpu.VMEM((STRATA, 3, SENT, UNITS), f32),
            pltpu.VMEM((ITEMS, UNITS), f32),
            pltpu.VMEM((ITEMS, UNITS), f32),
            pltpu.VMEM((ROUTED, UNITS), f32),
            pltpu.VMEM((4, QUARTER, UNITS), jnp.bfloat16),
            pltpu.VMEM((ITEMS, UNITS), jnp.bfloat16),
            pltpu.VMEM((ITEMS, UNITS), f32),
            pltpu.VMEM((QUARTER, UNITS), f32),
            dma((STRATA + 3,)),
            dma((STRATA,)),
            dma((STRATA, len(PARTS), SLOTS)),
            dma((STRATA,)),
            dma((STRATA, PIECES)),
            dma((STRATA,)),
            dma((STRATA, PIECES)),
            dma((STRATA,)),
            dma((STRATA,)),
            dma,
            dma,
        ],
        compiler_params=pltpu.CompilerParams(
            collective_id=number, has_side_effects=True, vmem_limit_bytes=63 << 20
        ),
        cost_estimate=pl.CostEstimate(
            flops=3 * 6 * USERS * ITEMS * UNITS, bytes_accessed=3 << 20, transcendentals=1 << 20
        ),
    )(matchings, interactions, user_shape, item_shape)


def per_device(interactions, matchings, user_shape, item_shape):
    calls = []
    for first in (0, Z1, Z2, Z2 | Z1):
        for second in (0, FAR):
            far = (first, first & FAR ^ second, second ^ FAR)
            calls.append(functools.partial(call, far, len(calls)))
    first, second = matchings[0] // Z1 & 3, matchings[1] // FAR & 1
    return lax.switch(
        first * 2 + second, calls, interactions, matchings, user_shape, item_shape
    )


def solution(mesh):
    placed = (P(None, "users", "items"), P(), P("users", None), P(("users", "items"), None))
    return jax.shard_map(
        per_device,
        mesh=mesh,
        in_specs=placed,
        out_specs=(P("users", None), P(("users", "items"), None)),
        check_vma=False,
    )
```

```python
import functools

import jax
import jax.numpy as jnp
from jax import lax
from jax.experimental import pallas as pl
from jax.experimental.pallas import tpu as pltpu
from jax.sharding import PartitionSpec as P

MESH = pl.DeviceIdType.MESH
STRATA = 3
UNITS = 128
USERS = 1280
ITEMS = 256
QUARTER = 320
PIECES = 4
PIECE = QUARTER // PIECES
SENT = QUARTER + 8
ROUTED = ITEMS + 8
FACTOR = 64.0
CORE, Z0, Z1, Z2, Y0, Y1 = 1, 2, 4, 8, 16, 32
HOME = 63
Y = Y0 | Y1
MASKS = (CORE, Z0, Z1, Y0, Y1, Y)
STAGES = 5
SLOTS = STAGES + 2
FAR = Z2
PARTS = (
    (0, 128, (FAR, Y, Z1, Z0, CORE)),
    (128, 136, (Y, Z0, Z1, FAR, CORE)),
)
STAGE_TIME = {CORE: 1.5, Z0: 4.4, Z1: 5.2, FAR: 10.5, Y: 7.5}
SCATTERED, SCATTER_STEP, EXCHANGED, EXCHANGE_STEP = 3.0, 1.7, 11.0, 3.5


def cotangent(x):
    r = x - jnp.floor(x + 0.5)
    s = r * r
    series = 1.2898681 + s * (
        0.16464647 + s * (0.034686124 + s * (0.0081547124 + s * (0.0019891502 + s * 0.00049217311)))
    )
    return (1.0 - 3.0 * s) / (r * (1.0 - s)) - r * series


def digamma_parts(x, positive=False):
    if positive:
        z = x
    else:
        negative = x <= 0.0
        z = jnp.where(negative, 1.0 - x, x)
    y = z + 4.0
    inverse = 1.0 / y
    square = inverse * inverse
    tail = 0.5 * inverse + square * (
        0.083333333 - square * (0.0083333333 - square * 0.003968254)
    )
    low = jnp.minimum(z, 1e8)
    p = low * (low + 3.0)
    e = -tail - (2.0 * low + 3.0) * (2.0 * p + 2.0) / (p * (p + 2.0))
    if not positive:
        e = jnp.where(negative, e - cotangent(x), e)
    return y, e


def inverse_rate(rte):
    return jnp.where(rte >= 0.0, 1.0 / rte, jnp.nan)


def exp_log(shp, rte, positive=False):
    y, e = digamma_parts(shp, positive)
    return y * inverse_rate(rte) * jnp.exp(e)


def log_mean(shp, rte):
    y, e = digamma_parts(shp)
    return jnp.log(y) + e - jnp.log(rte)


def in_rows(count, step, body):
    def once(n, carry):
        body(pl.ds(pl.multiple_of(n * step, step), step))
        return carry

    lax.fori_loop(0, count // step, once, 0)


def rows8(row):
    return jnp.broadcast_to(row, (8, UNITS))


def column_sum(value):
    return jnp.sum(value, axis=0, keepdims=True)


def kernel(
    far, match_hbm, inter_hbm, user_hbm, item_hbm, ulog_ref, ilog_ref,
    match_ref, inter, user_ref, item_ref,
    route_src, route_dst, rs_src, rs_dst, zh_src, zh_dst, ag_src, ag_dst, fin_src, fin_dst,
    visit, uexp, iexp, istat, ushp,
    load_sem, route_ss, route_rs, rs_ss, rs_rs, zh_ss, zh_rs, ag_ss, ag_rs, fin_ss, fin_rs,
):
    u = lax.axis_index("users")
    i = lax.axis_index("items")
    x = i // 2

    def at_user(mask):
        return (u ^ mask, i)

    def at_x(step):
        return (u, (i + 2 * step) % 8)

    at_zh = (u, i ^ 1)

    barrier = pltpu.get_barrier_semaphore()
    moves = MASKS + (HOME,) + tuple(sorted(set(far) - {0, Z1}))
    partners = [at_user(mask) for mask in moves] + [at_x(1), at_x(2), at_x(3), at_zh]
    for partner in partners:
        pl.semaphore_signal(barrier, inc=1, device_id=partner, device_id_type=MESH)

    load_item = pltpu.make_async_copy(item_hbm, item_ref, load_sem.at[STRATA])
    load_user = pltpu.make_async_copy(user_hbm, user_ref, load_sem.at[STRATA + 1])
    load_match = pltpu.make_async_copy(match_hbm, match_ref, load_sem.at[STRATA + 2])
    loads = [
        pltpu.make_async_copy(inter_hbm.at[s], inter.at[s], load_sem.at[s]) for s in range(STRATA)
    ]
    for load in [load_item, load_match, load_user] + loads:
        load.start()

    def remote(src, dst, ss, rs, device):
        return pltpu.make_async_remote_copy(
            src_ref=src, dst_ref=dst, send_sem=ss, recv_sem=rs, device_id=device, device_id_type=MESH
        )

    def route_part(s, part):
        first, rows, order = PARTS[part]
        masks = tuple(far[s] if mask == FAR else mask for mask in order if s or mask != Z1)
        return first, rows, tuple(mask for mask in masks if mask)

    def known(s, mask):
        return mask & (FAR if s else FAR | Z1)

    def route_copies(s, part, stage):
        first, rows, order = route_part(s, part)
        rows = pl.ds(first, rows)
        masks = (Y0, Y1, Y) if order[stage] == Y else (order[stage],)
        slots = (stage, STAGES, STAGES + 1)
        return [
            remote(
                route_src.at[s, stage, rows], route_dst.at[s, slot, rows], route_ss.at[s],
                route_rs.at[s, part, slot], at_user(mask),
            )
            for mask, slot in zip(masks, slots)
        ]

    def route_start(s, part, stage):
        for copy in route_copies(s, part, stage):
            copy.start()

    def rs_rows(piece):
        return pl.ds(8 + piece * PIECE, PIECE) if piece else pl.ds(0, 8 + PIECE)

    def rs_copy(s, step, piece):
        rows = rs_rows(piece)
        return remote(
            rs_src.at[s, step, rows], rs_dst.at[s, step - 1, rows], rs_ss.at[s],
            rs_rs.at[s, piece], at_x(step),
        )

    def zh_copy(s, piece):
        rows = rs_rows(piece)
        return remote(
            zh_src.at[s, rows], zh_dst.at[s, rows], zh_ss.at[s], zh_rs.at[s, piece], at_zh
        )

    def ag_copy(s, step, piece):
        more = 8 if piece == PIECES - 1 else 0
        rows = pl.ds(piece * PIECE, PIECE + more)
        return remote(
            ag_src.at[s, rows], ag_dst.at[s, step - 1, rows], ag_ss.at[s], ag_rs.at[s], at_x(step),
        )

    def wait_bytes(ref, sem):
        pltpu.make_async_copy(ref, ref, sem).wait()

    def routed(s):
        events = []
        for part in range(len(PARTS)):
            at = 0.0
            for stage, mask in enumerate(route_part(s, part)[2]):
                at += STAGE_TIME.get(mask, STAGE_TIME[FAR])
                events.append((at, functools.partial(route_next, s, part, stage)))
        return events

    def run(events):
        for _, event in sorted(events, key=lambda timed: timed[0]):
            event()

    def route_next(s, part, stage):
        first, rows, order = route_part(s, part)
        rows = pl.ds(first, rows)
        for copy in route_copies(s, part, stage):
            copy.wait_recv()
        if known(s, order[stage]):
            value = route_dst[s, stage, rows]
        else:
            m0, m1 = match_ref[0], match_ref[1]
            mask = (m0, m0 ^ m1, m1 ^ HOME)[s]
            picked = mask & order[stage]
            value = jnp.where(picked != 0, route_dst[s, stage, rows], route_src[s, stage, rows])
            if order[stage] == Y:
                value = jnp.where(picked == Y1, route_dst[s, STAGES, rows], value)
                value = jnp.where(picked == Y, route_dst[s, STAGES + 1, rows], value)
        if stage + 1 < len(order):
            route_src[s, stage + 1, rows] = value
            route_start(s, part, stage + 1)
        else:
            visit[rows] = value

    load_item.wait()
    route_src[0, 0, 0:ITEMS] = item_ref[...].astype(jnp.float32)
    route_src[0, 0, ITEMS:] = jnp.ones((8, UNITS), jnp.float32)
    load_match.wait()
    load_user.wait()

    pl.semaphore_wait(barrier, len(partners))
    for part in range(len(PARTS)):
        route_start(0, part, 0)

    def first_users(n, total):
        d, first = n // 5, pl.multiple_of((n % 5) * 64, 64)
        shp = user_ref[pl.ds(((x + d) % 4) * QUARTER + first, 64), :].astype(jnp.float32)
        uexp[d, pl.ds(first, 64)] = exp_log(
            shp, jnp.ones((1, UNITS), jnp.float32), True
        ).astype(jnp.bfloat16)
        return total + column_sum(shp)

    theta = lax.fori_loop(0, 20, first_users, jnp.zeros((1, UNITS), jnp.float32))
    ushp[...] = user_ref[pl.ds(x * QUARTER, QUARTER), :].astype(jnp.float32)
    urte = jnp.ones((1, UNITS), jnp.float32)

    run(routed(0))

    for s in range(STRATA):
        last = s == STRATA - 1
        rte = visit[ITEMS : ITEMS + 1]

        def item_rows(rows):
            iexp[rows] = exp_log(visit[rows], rte).astype(jnp.bfloat16)

        in_rows(ITEMS, 64, item_rows)
        rs_src[s, :, 0:8] = jnp.broadcast_to(column_sum(visit[0:ITEMS]) / rte, (4, 8, UNITS))
        istat[...] = jnp.zeros_like(istat)
        loads[s].wait()

        def users_of(d, first, rows):
            weights = inter[s, pl.ds(((x + d) % 4) * QUARTER + first, rows), :]
            ue = uexp[d, pl.ds(first, rows)]
            ie = iexp[...]
            denominator = lax.dot_general(
                ue, ie, (((1,), (1,)), ((), ())), preferred_element_type=jnp.float32
            )
            ratios = (weights.astype(jnp.float32) / denominator).astype(jnp.bfloat16)
            rs_src[s, d, pl.ds(8 + first, rows)] = ue.astype(jnp.float32) * jnp.dot(
                ratios, ie, preferred_element_type=jnp.float32
            )
            istat[...] += lax.dot_general(
                ratios, ue, (((0,), (0,)), ((), ())), preferred_element_type=jnp.float32
            )

        def users_sent(n, carry):
            d, half = (n + 1) % 4, n // 4
            users_of(d, pl.multiple_of(half * (QUARTER // 2), 32), QUARTER // 2)
            for step in range(2):
                @pl.when((d > 0) & (half == step))
                def _(step=step):
                    for piece in range(step * PIECES // 2, (step + 1) * PIECES // 2):
                        rs_copy(s, d, piece).start()

            return carry

        lax.fori_loop(0, 8, users_sent, 0)

        new_rte = 0.5 * rte + 0.5 * (0.3 + FACTOR * theta)

        def new_rows(rows):
            stat = iexp[rows].astype(jnp.float32) * istat[rows]
            shp = 0.5 * visit[rows] + 0.5 * (0.3 + FACTOR * stat)
            if last:
                fin_src[rows] = log_mean(shp, new_rte)
            else:
                route_src[s + 1, 0, rows] = shp

        in_rows(ITEMS, 64, new_rows)
        if last:
            final = remote(fin_src, fin_dst, fin_ss, fin_rs, at_user(HOME))
            final.start()
        else:
            route_src[s + 1, 0, ITEMS:] = rows8(new_rte)
            for part in range(len(PARTS)):
                route_start(s + 1, part, 0)

        state = {"urte": urte, "columns": jnp.zeros((1, UNITS), jnp.float32)}

        def scattered(piece):
            rows = rs_rows(piece)
            wait_bytes(rs_dst.at[s, :, rows], rs_rs.at[s, piece])
            zh_src[s, rows] = (rs_src[s, 0, rows] + rs_dst[s, 0, rows]) + (
                rs_dst[s, 1, rows] + rs_dst[s, 2, rows]
            )
            zh_copy(s, piece).start()

        def exchanged(piece):
            zh_copy(s, piece).wait_recv()
            if piece == 0:
                beta = zh_src[s, 0:1] + zh_dst[s, 0:1]
                state["urte"] = 0.5 * state["urte"] + 0.5 * (0.3 + FACTOR * beta)
            step = PIECE // 2

            def own_rows(n, columns):
                at = pl.multiple_of(piece * PIECE + n * step, 8)
                mine, stat = pl.ds(at, step), pl.ds(at + 8, step)
                total = zh_src[s, stat] + zh_dst[s, stat]
                own = 0.5 * ushp[mine] + 0.5 * (0.3 + FACTOR * total)
                ushp[mine] = own
                ag_src[s, mine] = (log_mean if last else exp_log)(own, state["urte"])
                return columns + column_sum(own)

            state["columns"] = lax.fori_loop(0, 2, own_rows, state["columns"])
            if piece == PIECES - 1:
                ag_src[s, QUARTER:] = rows8(state["columns"] / state["urte"])
            for step in range(1, 4):
                ag_copy(s, step, piece).start()

        events = [] if last else routed(s + 1)
        for piece in range(PIECES):
            events.append((SCATTERED + piece * SCATTER_STEP, functools.partial(scattered, piece)))
            events.append((EXCHANGED + piece * EXCHANGE_STEP, functools.partial(exchanged, piece)))
        run(events)
        urte = state["urte"]

        if last:
            final.wait_recv()
            ilog_ref[...] = fin_dst[...].astype(jnp.bfloat16)
            ulog_ref[pl.ds(x * QUARTER, QUARTER), :] = ag_src[s, 0:QUARTER].astype(jnp.bfloat16)
        else:
            uexp[0] = ag_src[s, 0:QUARTER].astype(jnp.bfloat16)
            theta = ag_src[s, QUARTER : QUARTER + 1]
        wait_bytes(ag_dst.at[s], ag_rs.at[s])
        for step in range(1, 4):
            value = ag_dst[s, step - 1, 0:QUARTER].astype(jnp.bfloat16)
            if last:
                ulog_ref[pl.ds(((x + 4 - step) % 4) * QUARTER, QUARTER), :] = value
            else:
                uexp[4 - step] = value
                theta = theta + ag_dst[s, step - 1, QUARTER : QUARTER + 1]

    for s in range(STRATA):
        wait_bytes(route_dst.at[s, 0 : len(route_part(s, 0)[2]) + 2], route_ss.at[s])
        wait_bytes(rs_src.at[s, 1:4], rs_ss.at[s])
        wait_bytes(zh_src.at[s], zh_ss.at[s])
        wait_bytes(ag_dst.at[s], ag_ss.at[s])
    final.wait_send()


def call(far, number, interactions, matchings, user_shape, item_shape):
    f32, dma = jnp.float32, pltpu.SemaphoreType.DMA
    vmem = pl.BlockSpec(memory_space=pltpu.VMEM)
    hbm = pl.BlockSpec(memory_space=pltpu.HBM)
    return pl.pallas_call(
        functools.partial(kernel, far),
        out_shape=(
            jax.ShapeDtypeStruct((USERS, UNITS), jnp.bfloat16),
            jax.ShapeDtypeStruct((ITEMS, UNITS), jnp.bfloat16),
        ),
        in_specs=[hbm, hbm, hbm, hbm],
        out_specs=(vmem, vmem),
        scratch_shapes=[
            pltpu.SMEM((STRATA,), jnp.int32),
            pltpu.VMEM((STRATA, USERS, ITEMS), jnp.bfloat16),
            pltpu.VMEM((USERS, UNITS), jnp.bfloat16),
            pltpu.VMEM((ITEMS, UNITS), jnp.bfloat16),
            pltpu.VMEM((STRATA, STAGES, ROUTED, UNITS), f32),
            pltpu.VMEM((STRATA, SLOTS, ROUTED, UNITS), f32),
            pltpu.VMEM((STRATA, 4, SENT, UNITS), f32),
            pltpu.VMEM((STRATA, 3, SENT, UNITS), f32),
            pltpu.VMEM((STRATA, SENT, UNITS), f32),
            pltpu.VMEM((STRATA, SENT, UNITS), f32),
            pltpu.VMEM((STRATA, SENT, UNITS), f32),
            pltpu.VMEM((STRATA, 3, SENT, UNITS), f32),
            pltpu.VMEM((ITEMS, UNITS), f32),
            pltpu.VMEM((ITEMS, UNITS), f32),
            pltpu.VMEM((ROUTED, UNITS), f32),
            pltpu.VMEM((4, QUARTER, UNITS), jnp.bfloat16),
            pltpu.VMEM((ITEMS, UNITS), jnp.bfloat16),
            pltpu.VMEM((ITEMS, UNITS), f32),
            pltpu.VMEM((QUARTER, UNITS), f32),
            dma((STRATA + 3,)),
            dma((STRATA,)),
            dma((STRATA, len(PARTS), SLOTS)),
            dma((STRATA,)),
            dma((STRATA, PIECES)),
            dma((STRATA,)),
            dma((STRATA, PIECES)),
            dma((STRATA,)),
            dma((STRATA,)),
            dma,
            dma,
        ],
        compiler_params=pltpu.CompilerParams(
            collective_id=number, has_side_effects=True, vmem_limit_bytes=63 << 20
        ),
        cost_estimate=pl.CostEstimate(
            flops=3 * 6 * USERS * ITEMS * UNITS, bytes_accessed=3 << 20, transcendentals=1 << 20
        ),
    )(matchings, interactions, user_shape, item_shape)


def per_device(interactions, matchings, user_shape, item_shape):
    calls = []
    for first in (0, Z1, Z2, Z2 | Z1):
        for second in (0, FAR):
            far = (first, first & FAR ^ second, second ^ FAR)
            calls.append(functools.partial(call, far, len(calls)))
    bits = (matchings // jnp.array((Z1, Z2, 1))) & jnp.array((3, 1, 0))
    chosen = jnp.sum(bits * jnp.array((2, 1, 0)))
    return lax.switch(chosen, calls, interactions, matchings, user_shape, item_shape)


def solution(mesh):
    placed = (P(None, "users", "items"), P(), P("users", None), P(("users", "items"), None))
    return jax.shard_map(
        per_device,
        mesh=mesh,
        in_specs=placed,
        out_specs=(P("users", None), P(("users", "items"), None)),
        check_vma=False,
    )
```
